512 devices in a mesh: blk: 128 (over x, z_hi, y, core), grp: 4 (over z_lo).
Axes of the slice: x: 4, y: 8, z: 8 (z_hi: 2, z_lo: 4; z = z_hi * 4 + z_lo), core: 2. Of those that a mesh axis runs over, the one named last changes fastest.
Arguments:
- source_emb: float32 [128, 512, 400], P('blk', 'grp'), may hold values from -1.2 to 1.2
- source_state: float32 [128, 512], P('blk', 'grp'), may hold values from 0.01 to 0.1
- target_emb: float32 [128, 512, 400], P('blk', 'grp'), may hold values from -1.2 to 1.2
- target_state: float32 [128, 512], P('blk', 'grp'), may hold values from 0.01 to 0.1
- relation_emb: float32 [512, 400], replicated, may hold values from 0.1 to 1.9
- relation_state: float32 [512], replicated, may hold values from 0.01 to 0.1
- source_ids: int32 [2, 128, 4, 512], P(None, 'blk', 'grp'), may hold values from 0 to 127
- target_ids: int32 [2, 128, 4, 512], P(None, 'blk', 'grp'), may hold values from 0 to 127
- relation_ids: int32 [2, 128, 4, 512], P(None, 'blk', 'grp'), may hold values from 0 to 511
- edge_counts: int32 [2, 128, 4], P(None, 'blk', 'grp'), may hold values from 128 to 512, as said below
- sample_ids: int32 [2, 128, 4, 1, 256], P(None, 'blk', 'grp'), may hold values from 0 to 127
Outputs:
- source_out: float32 [128, 512, 400], P('blk', 'grp')
- source_state_out: float32 [128, 512], P('blk', 'grp')
- target_out: float32 [128, 512, 400], P('blk', 'grp')
- target_state_out: float32 [128, 512], P('blk', 'grp')
- relation_out: float32 [512, 400], replicated
- relation_state_out: float32 [512], replicated
The draws below stay inside these ranges and needn't reach their ends.
Inputs may be any that keep to these rules, and one draw needn't show every extreme that they name: `edge_counts`: in every round some bucket is full.
All inputs are finite; a program needn't handle non-finite values.
Results may differ from the reference program's by a relative error of at most 0.0003.
Values sent between devices are 32-bit elements; how exact they have to be, the bound alone decides.
No kernel may reach another device: no remote copies, remote signals or barrier semaphores. Data moves between devices by JAX's collectives and lax.ppermute only.
A program may use at most 64 MiB of HBM per device.

```python
import math
import jax
import jax.numpy as jnp
import numpy as np
from jax import lax

D = 400
RELATIONS = 512
ROWS_DEV = 128
NEGATIVES = 256
BLOCKS = 1
ROUNDS = 2
EDGE_SLOTS = 512
PARTS_SIZE = 128
GROUPS = 4
ROWS = 512


def draw_edge_counts(key, part):
    key = jax.random.fold_in(key, 11)
    first_key, second_key = jax.random.split(key)
    dims_shape = (ROUNDS, PARTS_SIZE, GROUPS)
    counted = jax.random.randint(first_key, dims_shape, EDGE_SLOTS // 4, EDGE_SLOTS + 1)
    chosen = jax.random.randint(second_key, (ROUNDS, 1, 1), 0, PARTS_SIZE * GROUPS)
    position = lax.broadcasted_iota(jnp.int32, dims_shape, 1) * GROUPS + lax.broadcasted_iota(jnp.int32, dims_shape, 2)
    return jnp.where(position == chosen, EDGE_SLOTS, counted).astype(jnp.int32)


def place_ends(values, key, least, top_value):
    longest = values.shape.index(max(values.shape))
    spots = []
    for shift in (0, 1):
        where = [jax.random.randint(jax.random.fold_in(key, axis), (), 0, length) for axis, length in enumerate(values.shape)]
        where[longest] = (where[longest] + shift) % values.shape[longest]
        spots.append(tuple(where))
    return values.at[spots[0]].set(least).at[spots[1]].set(top_value)


def block_scale(own_key, extent, cuts, least, high):
    level, own = 1.0, jax.random.fold_in(own_key, 6)
    for dim, shards_of in cuts:
        draws = jnp.exp(jax.random.uniform(jax.random.fold_in(own, dim), (shards_of,), jnp.float32, least / len(cuts), high / len(cuts)))
        level = level * jnp.repeat(draws, extent[dim] // shards_of).reshape([-1 if axis == dim else 1 for axis in range(len(extent))])
    return level


def rank_table(count, lean):
    portions = [(1 << 20) // math.isqrt(grade ** lean) + 1 for grade in range(1, count + 1)]
    deviation = 1 + sum(portions) // (1 << 30)
    return np.cumsum(np.array([max(1, weight // deviation) for weight in portions]))


def skewed_ids(rng, shape, amount, slope):
    table = rank_table(amount, slope)
    pick = jax.random.randint(jax.random.fold_in(rng, 1), shape, 0, int(table[amount - 1]))
    rank = jnp.searchsorted(jnp.asarray(table, jnp.int32), pick, side="right")
    return jax.random.permutation(jax.random.fold_in(rng, 2), amount)[rank].astype(jnp.int32)


def bell_draw(key, dims, deviation, limit, shards=(), kind=jnp.bfloat16):
    entries = deviation * jax.random.normal(key, dims, jnp.float32)
    if shards:
        entries = entries * block_scale(key, dims, shards, -0.22, 0.18)
    return jnp.clip(entries, -limit, limit).astype(kind)


def setup_inputs(seed: int = 0) -> dict:
    streams_of = jax.random.split(jax.random.key(seed), 12)
    return {
        "source_emb": bell_draw(streams_of[0], (PARTS_SIZE, ROWS, D), 0.2, 1.2, ((0, 128), (1, 4)), jnp.float32),
        "source_state": jnp.clip(jnp.exp(math.log(0.1) - 2.3025851 * jax.random.uniform(streams_of[1], (PARTS_SIZE, ROWS), jnp.float32) ** block_scale(streams_of[1], (PARTS_SIZE, ROWS), ((0, 128), (1, 4)), -0.2, 0.2)), 0.01, 0.1),
        "target_emb": bell_draw(streams_of[2], (PARTS_SIZE, ROWS, D), 0.2, 1.2, ((0, 128), (1, 4)), jnp.float32),
        "target_state": jnp.clip(jnp.exp(math.log(0.1) - 2.3025851 * jax.random.uniform(streams_of[3], (PARTS_SIZE, ROWS), jnp.float32) ** block_scale(streams_of[3], (PARTS_SIZE, ROWS), ((0, 128), (1, 4)), -0.2, 0.2)), 0.01, 0.1),
        "relation_emb": jnp.clip(1.0 + 0.18 * jax.random.normal(streams_of[4], (RELATIONS, D), jnp.float32), 0.1, 1.9),
        "relation_state": jnp.clip(jnp.exp(jax.random.uniform(streams_of[5], (RELATIONS,), jnp.float32, math.log(0.01), math.log(0.1))), 0.01, 0.1),
        "source_ids": place_ends(jax.random.randint(streams_of[6], (ROUNDS, PARTS_SIZE, GROUPS, EDGE_SLOTS), 0, ROWS_DEV), jax.random.fold_in(streams_of[6], 1), 0, ROWS_DEV - 1).astype(jnp.int32),
        "target_ids": place_ends(jax.random.randint(streams_of[7], (ROUNDS, PARTS_SIZE, GROUPS, EDGE_SLOTS), 0, ROWS_DEV), jax.random.fold_in(streams_of[7], 1), 0, ROWS_DEV - 1).astype(jnp.int32),
        "relation_ids": place_ends(skewed_ids(streams_of[8], (ROUNDS, PARTS_SIZE, GROUPS, EDGE_SLOTS), RELATIONS, 2), jax.random.fold_in(streams_of[8], 3), 0, RELATIONS - 1).astype(jnp.int32),
        "edge_counts": draw_edge_counts(jax.random.fold_in(streams_of[11], 71), 0),
        "sample_ids": place_ends(jax.random.randint(streams_of[10], (ROUNDS, PARTS_SIZE, GROUPS, BLOCKS, NEGATIVES), 0, ROWS_DEV), jax.random.fold_in(streams_of[10], 1), 0, ROWS_DEV - 1).astype(jnp.int32),
    }


learning_rate = 0.1
relation_rate = 0.1

def adagrad(weights, accum, grads, rate):
    fresh = accum + lax.optimization_barrier(jnp.mean(grads * grads, axis=-1))
    return (weights - rate * grads * lax.rsqrt(fresh)[..., None], fresh)

def bucket(source_rows, target_rows, relation, source_idx, target_idx, kind_idx, live_count, sample_idx):
    slots = source_idx.shape[0]
    blocks, samples = sample_idx.shape
    per_block = slots // blocks
    width = source_rows.shape[1]
    nrows = source_rows.shape[0]
    alive = (jnp.arange(slots, dtype=jnp.int32) < live_count).astype(jnp.float32)
    left = source_rows[source_idx]
    right = target_rows[target_idx]
    scale = relation[kind_idx]
    query = left * scale
    positive = lax.optimization_barrier(jnp.sum(query * right, axis=-1))
    sampled = target_rows[sample_idx]
    blocked = query.reshape(blocks, per_block, width)
    negative = jnp.einsum('bid,bjd->bij', blocked, sampled, precision=lax.Precision.HIGHEST)
    pull = -alive * jax.nn.sigmoid(-positive)
    push = alive.reshape(blocks, per_block, 1) * jax.nn.sigmoid(negative) / samples
    grad_query = pull[:, None] * right + jnp.einsum('bij,bjd->bid', push, sampled, precision=lax.Precision.HIGHEST).reshape(slots, width)
    grad_source = jax.ops.segment_sum(grad_query * scale, source_idx, num_segments=nrows)
    to_samples = jnp.einsum('bij,bid->bjd', push, blocked, precision=lax.Precision.HIGHEST).reshape(-1, width)
    grad_target = jax.ops.segment_sum(pull[:, None] * query, target_idx, num_segments=nrows)
    grad_target = grad_target + jax.ops.segment_sum(to_samples, sample_idx.reshape(-1), num_segments=nrows)
    grad_relation = jax.ops.segment_sum(grad_query * left, kind_idx, num_segments=relation.shape[0])
    return (grad_source, grad_target, grad_relation)

def reference(source_emb, source_state, target_emb, target_state, relation_emb, relation_state, source_ids, target_ids, relation_ids, edge_counts, sample_ids):
    parts = source_emb.shape[0]
    slabs = parts * GROUPS
    width = source_emb.shape[2]
    source_rows = source_emb.reshape(slabs, ROWS_DEV, width)
    source_acc = source_state.reshape(slabs, ROWS_DEV)
    target_rows = target_emb.reshape(slabs, ROWS_DEV, width)
    target_acc = target_state.reshape(slabs, ROWS_DEV)
    flat_source = source_ids.reshape(ROUNDS, slabs, -1)
    flat_target = target_ids.reshape(ROUNDS, slabs, -1)
    flat_kind = relation_ids.reshape(ROUNDS, slabs, -1)
    flat_count = edge_counts.reshape(ROUNDS, slabs)
    flat_sample = sample_ids.reshape(ROUNDS, slabs, BLOCKS, NEGATIVES)
    total = jnp.zeros(relation_emb.shape, jnp.float32)
    for round_index in range(ROUNDS):

        def visit(running, inputs):
            grad_source, grad_target, grad_relation = bucket(inputs[0], inputs[1], relation_emb, inputs[2], inputs[3], inputs[4], inputs[5], inputs[6])
            return (running + grad_relation, (grad_source, grad_target))
        total, grads = lax.scan(visit, total, (source_rows, target_rows, flat_source[round_index], flat_target[round_index], flat_kind[round_index], flat_count[round_index], flat_sample[round_index]))
        target_rows, target_acc = adagrad(target_rows, target_acc, grads[1], learning_rate)
        source_rows, source_acc = adagrad(source_rows, source_acc, grads[0], learning_rate)
        if round_index + 1 < ROUNDS:
            source_rows = jnp.roll(source_rows.reshape(parts, GROUPS, ROWS_DEV, width), 1, axis=0).reshape(slabs, ROWS_DEV, width)
            source_acc = jnp.roll(source_acc.reshape(parts, GROUPS, ROWS_DEV), 1, axis=0).reshape(slabs, ROWS_DEV)
    relation_out, relation_state_out = adagrad(relation_emb, relation_state, total, relation_rate)
    return (source_rows.reshape(source_emb.shape), source_acc.reshape(source_state.shape), target_rows.reshape(target_emb.shape), target_acc.reshape(target_state.shape), relation_out, relation_state_out)
```

```python
import functools

import jax
import jax.numpy as jnp
import numpy as np
from jax import lax
from jax.experimental import pallas as pl
from jax.experimental.pallas import tpu as pltpu
from jax.sharding import Mesh
from jax.sharding import PartitionSpec as P

learning_rate = 0.1
relation_rate = 0.1

SIZES = (4, 2, 8, 2, 4)
AXES = ("x", "h", "y", "c", "l")
BLK = ("x", "h", "y", "c")
F32 = jnp.float32
VM = pl.BlockSpec(memory_space=pltpu.VMEM)
LANES = 128
TILES = 50
OWNERS = 16
FIRST = [TILES * d // OWNERS for d in range(OWNERS)] + [TILES]


def place(x, h, y, c, l):
    return (((x * 2 + h) * 8 + y) * 2 + c) * 4 + l


def plane_groups():
    first = [[place(x, h, y, 0, l) for x in range(4) for y in range(8)] for h in range(2) for l in range(4)]
    second = [[place(x, h, y, 1, l) for x in range(4) for h in range(2) for l in range(4)] for y in range(8)]
    return first + second


def line_groups():
    first = [[place(x, h, y, 0, l) for h in range(2) for l in range(4)] for x in range(4) for y in range(8)]
    second = [[place(x, h, y, 1, l) for y in range(8)] for x in range(4) for h in range(2) for l in range(4)]
    return first + second


def split(value):
    high = value.astype(jnp.bfloat16)
    return high, (value - high.astype(F32)).astype(jnp.bfloat16)


def product(left, right, dims=((1,), (0,))):
    return lax.dot_general(left, right, (dims, ((), ())), preferred_element_type=F32)


def product3(left, right, dims=((1,), (0,))):
    lh, ll = left
    rh, rl = right
    return product(lh, rh, dims) + product(lh, rl, dims) + product(ll, rh, dims)


def one_hot(ids, count):
    rows = lax.broadcasted_iota(jnp.int32, (count, ids.shape[1]), 0)
    return (rows == ids).astype(F32).astype(jnp.bfloat16)


def gather(table, hot):
    high, low = split(table)
    if high.shape[1] == LANES:
        return product(jnp.concatenate([high, low], 1), jnp.concatenate([hot, hot], 0))
    return product(high, hot) + product(low, hot)


def scatter(values, hot):
    high, low = split(values)
    across = ((1,), (1,))
    return product(high, hot, across) + product(low, hot, across)


def adagrad(weights, accum, grads, rate):
    fresh = accum + jnp.sum(grads * grads, axis=0, keepdims=True) / grads.shape[0]
    return weights - rate * grads * lax.rsqrt(fresh), fresh


def scores(query, right, sampled, count):
    slots, negatives = query.shape[1], sampled.shape[1]
    alive = (lax.broadcasted_iota(jnp.int32, (1, slots), 1) < count).astype(F32)
    positive = jnp.sum(query * right, axis=0, keepdims=True)
    negative = product3(split(sampled.T), split(query))
    pull = -alive * jax.nn.sigmoid(-positive)
    push = jax.nn.sigmoid(negative) * (alive / negatives)
    return pull, push


def target_grads(query, pull, push, target_hot, sample_hot):
    to_samples = product3(split(query), split(push), ((1,), (1,)))
    return scatter(pull * query, target_hot) + scatter(to_samples, sample_hot)


def first_edges(
    source, source_acc, target, relation, sid, tid, kid, nid, cnt,
    moved, query_out, pull_out, push_out, typed_out,
):
    left = gather(source[...], one_hot(sid[0, 0], LANES))
    right = gather(target[...], one_hot(tid[0, 0], LANES))
    sampled = gather(target[...], one_hot(nid[0, 0, 0], LANES))
    scale = gather(relation[...], one_hot(kid[0, 0], relation.shape[1]))
    query = left * scale
    pull, push = scores(query, right, sampled, cnt[0, 0, 0])
    grad_query = pull * right + product3(split(sampled), split(push))
    grads = scatter(grad_query * scale, one_hot(sid[0, 0], LANES))
    rows, acc = adagrad(source[...], source_acc[...], grads, learning_rate)
    width = source.shape[0]
    moved[0:width, :] = rows
    moved[width : width + 8, :] = jnp.broadcast_to(acc, (8, LANES))
    query_out[...] = query
    pull_out[...] = pull
    push_out[...] = push
    typed_out[...] = grad_query * left


def first_rest(
    target, target_acc, relation, tid, kid, nid, query, pull, push, typed,
    target_out, target_acc_out, total, right_out, sampled_out, scale_out,
):
    grads = target_grads(
        query[...], pull[...], push[...], one_hot(tid[0, 0], LANES), one_hot(nid[0, 0, 0], LANES)
    )
    rows, acc = adagrad(target[...], target_acc[...], grads, learning_rate)
    target_out[...] = rows
    target_acc_out[...] = acc
    sums = scatter(typed[...], one_hot(kid[0, 0], relation.shape[1]))
    half = sums.shape[1] // 2
    total[0] = sums[:, :half]
    total[1] = sums[:, half:]
    right_out[...] = gather(rows, one_hot(tid[1, 0], LANES))
    sampled_out[...] = gather(rows, one_hot(nid[1, 0, 0], LANES))
    scale_out[...] = gather(relation[...], one_hot(kid[1, 0], relation.shape[1]))


def put_blocks(out, sums):
    for block in range(2):
        lanes = slice(block * LANES, (block + 1) * LANES)
        for d in range(OWNERS):
            row = FIRST[d] * 8
            out[block * OWNERS + d] = sums[row : row + 32, lanes]


def second_edges(
    moved, right, sampled, scale, sid, kid, cnt, total,
    query_out, pull_out, push_out, grad_out, typed_out, sent,
):
    width = right.shape[0]
    left = gather(moved[0:width, :], one_hot(sid[1, 0], LANES))
    query = left * scale[...]
    pull, push = scores(query, right[...], sampled[...], cnt[1, 0, 0])
    grad_query = pull * right[...] + product3(split(sampled[...]), split(push))
    typed = grad_query * left
    other = 1 - lax.axis_index("c")
    half = total.shape[2]
    put_blocks(sent, total[other] + scatter(typed, one_hot(kid[1, 0] - other * half, half)))
    query_out[...] = query
    pull_out[...] = pull
    push_out[...] = push
    grad_out[...] = grad_query
    typed_out[...] = typed


def second_rest(
    moved, target, target_acc, scale, sid, tid, kid, nid, query, pull, push, grad_query, typed, total,
    source_out, source_acc_out, target_out, target_acc_out, kept,
):
    width = target.shape[0]
    me = lax.axis_index("c")
    half = total.shape[2]
    put_blocks(kept, total[me] + scatter(typed[...], one_hot(kid[1, 0] - me * half, half)))
    grads = target_grads(
        query[...], pull[...], push[...], one_hot(tid[1, 0], LANES), one_hot(nid[1, 0, 0], LANES)
    )
    target_out[...], target_acc_out[...] = adagrad(target[...], target_acc[...], grads, learning_rate)
    grads = scatter(grad_query[...] * scale[...], one_hot(sid[1, 0], LANES))
    source_out[...], source_acc_out[...] = adagrad(
        moved[0:width, :], moved[width : width + 1, :], grads, learning_rate
    )


def last_update(mine, theirs, relation, relation_acc, relation_out, relation_acc_out):
    me = lax.axis_index("c")
    for blocks, half in ((mine, me), (theirs, 1 - me)):
        for block in range(2):
            lanes = pl.ds(pl.multiple_of((half * 2 + block) * LANES, LANES), LANES)
            pieces = [
                blocks[block * OWNERS + d, 0 : (FIRST[d + 1] - FIRST[d]) * 8, :] for d in range(OWNERS)
            ]
            grads = jnp.concatenate(pieces, 0)
            relation_out[:, lanes], relation_acc_out[:, lanes] = adagrad(
                relation[:, lanes], relation_acc[:, lanes], grads, relation_rate
            )


def call(kernel, shapes, *operands, flops=0):
    moved = sum(4 * int(np.prod(s)) for s in shapes) + sum(4 * o.size for o in operands)
    return pl.pallas_call(
        kernel,
        out_shape=[jax.ShapeDtypeStruct(s, F32) for s in shapes],
        in_specs=[VM] * len(operands),
        out_specs=[VM] * len(shapes),
        compiler_params=pltpu.CompilerParams(vmem_limit_bytes=40 * 2**20),
        cost_estimate=pl.CostEstimate(flops=flops, bytes_accessed=moved, transcendentals=0),
    )(*operands)


def exchange(blocks, groups):
    return lax.all_to_all(blocks, AXES, 0, 0, axis_index_groups=groups, tiled=True)


def spread(block, count):
    return jnp.broadcast_to(block[None], (count,) + block.shape)


def swap_cores(value):
    return lax.ppermute(value, "c", [(0, 1), (1, 0)])


def on_device(
    source_emb, source_state, target_emb, target_state, relation_emb, relation_state,
    sid, tid, kid, cnt, nid,
):
    source, target, relation = source_emb[0].T, target_emb[0].T, relation_emb.T
    width, kinds = relation.shape
    slots, negatives = sid.shape[-1], nid.shape[-1]
    table, row = (width, LANES), (1, LANES)
    edges, pairs = (width, slots), (negatives, slots)
    blocks = (2 * OWNERS, 32, LANES)
    work = 10**9
    moved, query, pull, push, typed = call(
        first_edges, [(width + 8, LANES), edges, (1, slots), pairs, edges],
        source, source_state, target, relation, sid, tid, kid, nid, cnt, flops=2 * work,
    )
    count = lax.axis_size(BLK)
    moved = lax.ppermute(moved, BLK, [(i, (i + 1) % count) for i in range(count)])
    target, target_acc, total, right, sampled, scale = call(
        first_rest, [table, row, (2, width, kinds // 2), edges, (width, negatives), edges],
        target, target_state, relation, tid, kid, nid, query, pull, push, typed, flops=2 * work,
    )
    query, pull, push, grad_query, typed, sent = call(
        second_edges, [edges, (1, slots), pairs, edges, edges, blocks],
        moved, right, sampled, scale, sid, kid, cnt, total, flops=2 * work,
    )
    received = swap_cores(sent)
    source, source_acc, target, target_acc, kept = call(
        second_rest, [table, row, table, row, blocks],
        moved, target, target_acc, scale, sid, tid, kid, nid, query, pull, push, grad_query, typed, total,
        flops=2 * work,
    )
    planes, lines = plane_groups(), line_groups()
    block = jnp.sum(exchange(kept + received, planes), 0)
    block = jnp.sum(exchange(spread(block, 8), lines), 0)
    mine = exchange(spread(block, 2 * OWNERS), planes)
    theirs = swap_cores(mine)
    relation, relation_acc = call(
        last_update, [(width, kinds), (1, kinds)], mine, theirs, relation, relation_state[None]
    )
    return (source.T[None], source_acc, target.T[None], target_acc, relation.T, relation_acc[0])


def solution(mesh):
    fine = Mesh(mesh.devices.reshape(SIZES), AXES)
    slab, sums = P(BLK, "l", None), P(BLK, "l")
    ids = P(None, BLK, "l", None)
    in_specs = (
        slab, sums, slab, sums, P(), P(), ids, ids, ids, P(None, BLK, "l"), P(None, BLK, "l", None, None),
    )
    out_specs = (slab, sums, slab, sums, P(), P())
    return jax.shard_map(
        on_device, mesh=fine, in_specs=in_specs, out_specs=out_specs, check_vma=False
    )
```

```python
import jax
import jax.numpy as jnp
import numpy as np
from jax import lax
from jax.experimental import pallas as pl
from jax.experimental.pallas import tpu as pltpu
from jax.sharding import Mesh
from jax.sharding import PartitionSpec as P

learning_rate = 0.1
relation_rate = 0.1

SIZES = (4, 2, 8, 2, 4)
AXES = ("x", "h", "y", "c", "l")
BLK = ("x", "h", "y", "c")
F32 = jnp.float32
VM = pl.BlockSpec(memory_space=pltpu.VMEM)
LANES = 128


def place(x, h, y, c, l):
    return (((x * 2 + h) * 8 + y) * 2 + c) * 4 + l


def plane_groups():
    first = [[place(x, h, y, 0, l) for x in range(4) for y in range(8)] for h in range(2) for l in range(4)]
    second = [[place(x, h, y, 1, l) for x in range(4) for h in range(2) for l in range(4)] for y in range(8)]
    return first + second


def line_groups():
    first = [[place(x, h, y, 0, l) for h in range(2) for l in range(4)] for x in range(4) for y in range(8)]
    second = [[place(x, h, y, 1, l) for y in range(8)] for x in range(4) for h in range(2) for l in range(4)]
    return first + second


def split(value):
    high = value.astype(jnp.bfloat16)
    return high, (value - high.astype(F32)).astype(jnp.bfloat16)


def product(left, right, dims=((1,), (0,))):
    return lax.dot_general(left, right, (dims, ((), ())), preferred_element_type=F32)


def product3(left, right, dims=((1,), (0,))):
    lh, ll = left
    rh, rl = right
    return product(lh, rh, dims) + product(lh, rl, dims) + product(ll, rh, dims)


def one_hot(ids, count):
    rows = lax.broadcasted_iota(jnp.int32, (count, ids.shape[1]), 0)
    return (rows == ids).astype(F32).astype(jnp.bfloat16)


def gather(table, hot):
    high, low = split(table)
    if high.shape[1] == LANES:
        return product(jnp.concatenate([high, low], 1), jnp.concatenate([hot, hot], 0))
    return product(high, hot) + product(low, hot)


def scatter(values, hot):
    high, low = split(values)
    across = ((1,), (1,))
    return product(high, hot, across) + product(low, hot, across)


def adagrad(weights, accum, grads, rate):
    fresh = accum + jnp.sum(grads * grads, axis=0, keepdims=True) / grads.shape[0]
    return weights - rate * grads * lax.rsqrt(fresh), fresh


def scores(query, right, sampled, count):
    slots, negatives = query.shape[1], sampled.shape[1]
    alive = (lax.broadcasted_iota(jnp.int32, (1, slots), 1) < count).astype(F32)
    positive = jnp.sum(query * right, axis=0, keepdims=True)
    negative = product3(split(sampled.T), split(query))
    pull = -alive * jax.nn.sigmoid(-positive)
    push = jax.nn.sigmoid(negative) * (alive / negatives)
    return pull, push


def target_grads(query, pull, push, target_hot, sample_hot):
    to_samples = product3(split(query), split(push), ((1,), (1,)))
    return scatter(pull * query, target_hot) + scatter(to_samples, sample_hot)


def bucket(source, target, scale, sid, tid, nid, cnt):
    left = gather(source, one_hot(sid, LANES))
    right = gather(target, one_hot(tid, LANES))
    sampled = gather(target, one_hot(nid, LANES))
    query = left * scale
    pull, push = scores(query, right, sampled, cnt)
    grad_query = pull * right + product3(split(sampled), split(push))
    return left, query, pull, push, grad_query


def first_source(
    kid_in, relation_in, sid_in, source_in, tid_in, target_in, nid_in, cnt_in, source_acc_in, moved,
    kid, relation, sid, source, tid, target, nid, cnt, source_acc, arrived,
):
    wanted = (
        (kid_in, kid), (relation_in, relation), (sid_in, sid), (source_in, source), (tid_in, tid),
        (target_in, target), (nid_in, nid), (cnt_in, cnt), (source_acc_in, source_acc),
    )
    copies = [pltpu.make_async_copy(a, b, arrived.at[i]) for i, (a, b) in enumerate(wanted)]
    for copy in copies:
        copy.start()
    copies[0].wait()
    kind_hot = one_hot(kid[0, 0], relation.shape[1])
    copies[1].wait()
    scale = gather(relation[...], kind_hot)
    for copy in copies[2:]:
        copy.wait()
    grad_query = bucket(
        source[...], target[...], scale, sid[0, 0], tid[0, 0], nid[0, 0, 0], cnt[0, :, 0:1]
    )[-1]
    grads = scatter(grad_query * scale, one_hot(sid[0, 0], LANES))
    rows, acc = adagrad(source[...], source_acc[...], grads, learning_rate)
    width = source.shape[0]
    moved[0:width, :] = rows
    moved[width : width + 8, :] = jnp.broadcast_to(acc, (8, LANES))


def first_rest(
    source, target, target_acc, relation, sid, tid, kid, nid, cnt,
    target_out, target_acc_out, total, right_out, sampled_out, scale_out,
):
    kind_hot = one_hot(kid[0, 0], relation.shape[1])
    left, query, pull, push, grad_query = bucket(
        source[...], target[...], gather(relation[...], kind_hot), sid[0, 0], tid[0, 0], nid[0, 0, 0],
        cnt[0, :, 0:1],
    )
    grads = target_grads(query, pull, push, one_hot(tid[0, 0], LANES), one_hot(nid[0, 0, 0], LANES))
    rows, acc = adagrad(target[...], target_acc[...], grads, learning_rate)
    target_out[...] = rows
    target_acc_out[...] = acc
    sums = scatter(grad_query * left, kind_hot)
    half = sums.shape[1] // 2
    total[0] = sums[:, :half]
    total[1] = sums[:, half:]
    right_out[...] = gather(rows, one_hot(tid[1, 0], LANES))
    sampled_out[...] = gather(rows, one_hot(nid[1, 0, 0], LANES))
    scale_out[...] = gather(relation[...], one_hot(kid[1, 0], relation.shape[1]))


def put_blocks(out, sums):
    width = sums.shape[0]
    for block in range(sums.shape[1] // LANES):
        out[block * width : (block + 1) * width, :] = sums[:, block * LANES : (block + 1) * LANES]


def second_edges(
    moved, right, sampled, scale, sid, kid, cnt, total,
    query_out, pull_out, push_out, grad_out, typed_out, sent,
):
    width = right.shape[0]
    left = gather(moved[0:width, :], one_hot(sid[1, 0], LANES))
    query = left * scale[...]
    pull, push = scores(query, right[...], sampled[...], cnt[0, :, 1:2])
    grad_query = pull * right[...] + product3(split(sampled[...]), split(push))
    typed = grad_query * left
    other = 1 - lax.axis_index("c")
    half = total.shape[2]
    put_blocks(sent, total[other] + scatter(typed, one_hot(kid[1, 0] - other * half, half)))
    query_out[...] = query
    pull_out[...] = pull
    push_out[...] = push
    grad_out[...] = grad_query
    typed_out[...] = typed


def second_rest(
    moved, target, target_acc, scale, sid, tid, kid, nid, query, pull, push, grad_query, typed, total,
    source_out, source_acc_out, target_out, target_acc_out, kept,
):
    width = target.shape[0]
    me = lax.axis_index("c")
    half = total.shape[2]
    put_blocks(kept, total[me] + scatter(typed[...], one_hot(kid[1, 0] - me * half, half)))
    grads = target_grads(
        query[...], pull[...], push[...], one_hot(tid[1, 0], LANES), one_hot(nid[1, 0, 0], LANES)
    )
    target_out[...], target_acc_out[...] = adagrad(target[...], target_acc[...], grads, learning_rate)
    grads = scatter(grad_query[...] * scale[...], one_hot(sid[1, 0], LANES))
    source_out[...], source_acc_out[...] = adagrad(
        moved[0:width, :], moved[width : width + 1, :], grads, learning_rate
    )


def last_update(sums, relation, relation_acc, relation_out, relation_acc_out):
    width, kinds = relation.shape
    for block in range(kinds // LANES):
        lanes = slice(block * LANES, (block + 1) * LANES)
        relation_out[:, lanes], relation_acc_out[:, lanes] = adagrad(
            relation[:, lanes], relation_acc[:, lanes], sums[block * width : (block + 1) * width, :], relation_rate
        )


def call(kernel, shapes, *operands, flops=0, fetch=False):
    scratch = []
    if fetch:
        scratch = [pltpu.VMEM(o.shape, o.dtype) for o in operands]
        scratch.append(pltpu.SemaphoreType.DMA((len(operands),)))
    moved = sum(4 * int(np.prod(s)) for s in shapes) + sum(4 * o.size for o in operands)
    return pl.pallas_call(
        kernel,
        out_shape=[jax.ShapeDtypeStruct(s, F32) for s in shapes],
        in_specs=[pl.BlockSpec(memory_space=pltpu.HBM) if fetch else VM] * len(operands),
        out_specs=[VM] * len(shapes),
        scratch_shapes=scratch,
        compiler_params=pltpu.CompilerParams(vmem_limit_bytes=(60 if fetch else 40) * 2**20),
        cost_estimate=pl.CostEstimate(flops=flops, bytes_accessed=moved, transcendentals=0),
    )(*operands)


def exchange(blocks, groups):
    return lax.all_to_all(blocks, AXES, 0, 0, axis_index_groups=groups, tiled=True)


def spread(block, count):
    return jnp.broadcast_to(block[None], (count,) + block.shape)


def swap_cores(value):
    return lax.ppermute(value, "c", [(0, 1), (1, 0)])


def on_device(
    source_emb, source_state, target_emb, target_state, relation_emb, relation_state,
    sid, tid, kid, cnt, nid,
):
    source, target, relation = source_emb[0].T, target_emb[0].T, relation_emb.T
    cnt = cnt.transpose(1, 2, 0)
    width, kinds = relation.shape
    slots, negatives = sid.shape[-1], nid.shape[-1]
    table, row = (width, LANES), (1, LANES)
    edges, pairs = (width, slots), (negatives, slots)
    blocks = (width * kinds // 2 // LANES, LANES)
    work = 10**9
    (moved,) = call(
        first_source, [(width + 8, LANES)],
        kid, relation, sid, source, tid, target, nid, cnt, source_state, flops=2 * work, fetch=True,
    )
    count = lax.axis_size(BLK)
    moved = lax.ppermute(moved, BLK, [(i, (i + 1) % count) for i in range(count)])
    target, target_acc, total, right, sampled, scale = call(
        first_rest, [table, row, (2, width, kinds // 2), edges, (width, negatives), edges],
        source, target, target_state, relation, sid, tid, kid, nid, cnt, flops=4 * work,
    )
    query, pull, push, grad_query, typed, sent = call(
        second_edges, [edges, (1, slots), pairs, edges, edges, blocks],
        moved, right, sampled, scale, sid, kid, cnt, total, flops=2 * work,
    )
    received = swap_cores(sent)
    source, source_acc, target, target_acc, kept = call(
        second_rest, [table, row, table, row, blocks],
        moved, target, target_acc, scale, sid, tid, kid, nid, query, pull, push, grad_query, typed, total,
        flops=2 * work,
    )
    planes, lines = plane_groups(), line_groups()
    in_plane, in_line = len(planes[0]), len(lines[0])
    block = jnp.sum(exchange((kept + received).reshape(in_plane, 1, -1), planes), 0)
    block = jnp.sum(exchange(spread(block, in_line), lines), 0)
    halves = exchange(spread(block, in_plane), planes).reshape(blocks)
    sums = lax.all_gather(halves, "c", tiled=True)
    relation, relation_acc = call(
        last_update, [(width, kinds), (1, kinds)], sums, relation, relation_state[None]
    )
    return (source.T[None], source_acc, target.T[None], target_acc, relation.T, relation_acc[0])


def solution(mesh):
    fine = Mesh(mesh.devices.reshape(SIZES), AXES)
    slab, sums = P(BLK, "l", None), P(BLK, "l")
    ids = P(None, BLK, "l", None)
    in_specs = (
        slab, sums, slab, sums, P(), P(), ids, ids, ids, P(None, BLK, "l"), P(None, BLK, "l", None, None),
    )
    out_specs = (slab, sums, slab, sums, P(), P())
    return jax.shard_map(
        on_device, mesh=fine, in_specs=in_specs, out_specs=out_specs, check_vma=False
    )
```

```python
import jax
import jax.numpy as jnp
import numpy as np
from jax import lax
from jax.experimental import pallas as pl
from jax.experimental.pallas import tpu as pltpu
from jax.sharding import Mesh
from jax.sharding import PartitionSpec as P

learning_rate = 0.1
relation_rate = 0.1

SIZES = (4, 2, 8, 2, 4)
AXES = ("x", "h", "y", "c", "l")
BLK = ("x", "h", "y", "c")
F32 = jnp.float32
VM = pl.BlockSpec(memory_space=pltpu.VMEM)
LANES = 128


def place(x, h, y, c, l):
    return (((x * 2 + h) * 8 + y) * 2 + c) * 4 + l


def plane_groups():
    first = [[place(x, h, y, 0, l) for x in range(4) for y in range(8)] for h in range(2) for l in range(4)]
    second = [[place(x, h, y, 1, l) for x in range(4) for h in range(2) for l in range(4)] for y in range(8)]
    return first + second


def line_groups():
    first = [[place(x, h, y, 0, l) for h in range(2) for l in range(4)] for x in range(4) for y in range(8)]
    second = [[place(x, h, y, 1, l) for y in range(8)] for x in range(4) for h in range(2) for l in range(4)]
    return first + second


def split(value):
    high = value.astype(jnp.bfloat16)
    return high, (value - high.astype(F32)).astype(jnp.bfloat16)


def product(left, right, dims=((1,), (0,))):
    return lax.dot_general(left, right, (dims, ((), ())), preferred_element_type=F32)


def product3(left, right, dims=((1,), (0,))):
    lh, ll = left
    rh, rl = right
    return product(lh, rh, dims) + product(lh, rl, dims) + product(ll, rh, dims)


def one_hot(ids, count):
    rows = lax.broadcasted_iota(jnp.int32, (count, ids.shape[1]), 0)
    return (rows == ids).astype(F32).astype(jnp.bfloat16)


def gather(table, hot):
    high, low = split(table)
    if high.shape[1] == LANES:
        return product(jnp.concatenate([high, low], 1), jnp.concatenate([hot, hot], 0))
    return product(high, hot) + product(low, hot)


def scatter(values, hot):
    high, low = split(values)
    across = ((1,), (1,))
    return product(high, hot, across) + product(low, hot, across)


def adagrad(weights, accum, grads, rate):
    fresh = accum + jnp.sum(grads * grads, axis=0, keepdims=True) / grads.shape[0]
    return weights - rate * grads * lax.rsqrt(fresh), fresh


def scores(query, right, sampled, count):
    slots, negatives = query.shape[1], sampled.shape[1]
    alive = (lax.broadcasted_iota(jnp.int32, (1, slots), 1) < count).astype(F32)
    positive = jnp.sum(query * right, axis=0, keepdims=True)
    negative = product3(split(sampled.T), split(query))
    pull = -alive * jax.nn.sigmoid(-positive)
    push = jax.nn.sigmoid(negative) * (alive / negatives)
    return pull, push


def target_grads(query, pull, push, target_hot, sample_hot):
    to_samples = product3(split(query), split(push), ((1,), (1,)))
    return scatter(pull * query, target_hot) + scatter(to_samples, sample_hot)


def bucket(left, right, sampled, scale, cnt):
    query = left * scale
    pull, push = scores(query, right, sampled, cnt)
    grad_query = pull * right + product3(split(sampled), split(push))
    return query, pull, push, grad_query


def first_source(*refs):
    count = (len(refs) - 2) // 2
    moved, arrived = refs[count], refs[-1]
    fetched = refs[count + 1 : -1]
    sid, source, tid, target, nid, kid, relation, cnt, source_acc = fetched[:9]
    copies = [pltpu.make_async_copy(refs[i], fetched[i], arrived.at[i]) for i in range(count)]
    for copy in copies:
        copy.start()
    for copy in copies:
        copy.wait()
    source_hot = one_hot(sid[0, 0], LANES)
    left = gather(source[...], source_hot)
    right = gather(target[...], one_hot(tid[0, 0], LANES))
    sampled = gather(target[...], one_hot(nid[0, 0, 0], LANES))
    scale = gather(relation[...], one_hot(kid[0, 0], relation.shape[1]))
    grad_query = bucket(left, right, sampled, scale, cnt[0, :, 0:1])[-1]
    grads = scatter(grad_query * scale, source_hot)
    rows, acc = adagrad(source[...], source_acc[...], grads, learning_rate)
    width = source.shape[0]
    moved[0:width, :] = rows
    moved[width : width + 8, :] = jnp.broadcast_to(acc, (8, LANES))


def first_rest(
    source, target, target_acc, relation, sid, tid, kid, nid, cnt,
    target_out, target_acc_out, total, right_out, sampled_out, scale_out,
):
    kind_hot = one_hot(kid[0, 0], relation.shape[1])
    target_hot, sample_hot = one_hot(tid[0, 0], LANES), one_hot(nid[0, 0, 0], LANES)
    left = gather(source[...], one_hot(sid[0, 0], LANES))
    query, pull, push, grad_query = bucket(
        left, gather(target[...], target_hot), gather(target[...], sample_hot), gather(relation[...], kind_hot),
        cnt[0, :, 0:1],
    )
    grads = target_grads(query, pull, push, target_hot, sample_hot)
    rows, acc = adagrad(target[...], target_acc[...], grads, learning_rate)
    target_out[...] = rows
    target_acc_out[...] = acc
    sums = scatter(grad_query * left, kind_hot)
    half = sums.shape[1] // 2
    total[0] = sums[:, :half]
    total[1] = sums[:, half:]
    right_out[...] = gather(rows, one_hot(tid[1, 0], LANES))
    sampled_out[...] = gather(rows, one_hot(nid[1, 0, 0], LANES))
    scale_out[...] = gather(relation[...], one_hot(kid[1, 0], relation.shape[1]))


def put_blocks(out, sums):
    width = sums.shape[0]
    for block in range(sums.shape[1] // LANES):
        out[block * width : (block + 1) * width, :] = sums[:, block * LANES : (block + 1) * LANES]


def second_edges(
    moved, right, sampled, scale, sid, kid, cnt, total,
    query_out, pull_out, push_out, grad_out, typed_out, sent,
):
    width = right.shape[0]
    left = gather(moved[0:width, :], one_hot(sid[1, 0], LANES))
    query = left * scale[...]
    pull, push = scores(query, right[...], sampled[...], cnt[0, :, 1:2])
    grad_query = pull * right[...] + product3(split(sampled[...]), split(push))
    typed = grad_query * left
    other = 1 - lax.axis_index("c")
    half = total.shape[2]
    put_blocks(sent, total[other] + scatter(typed, one_hot(kid[1, 0] - other * half, half)))
    query_out[...] = query
    pull_out[...] = pull
    push_out[...] = push
    grad_out[...] = grad_query
    typed_out[...] = typed


def second_rest(
    moved, target, target_acc, scale, sid, tid, kid, nid, query, pull, push, grad_query, typed, total,
    source_out, source_acc_out, target_out, target_acc_out, kept,
):
    width = target.shape[0]
    me = lax.axis_index("c")
    half = total.shape[2]
    put_blocks(kept, total[me] + scatter(typed[...], one_hot(kid[1, 0] - me * half, half)))
    grads = target_grads(
        query[...], pull[...], push[...], one_hot(tid[1, 0], LANES), one_hot(nid[1, 0, 0], LANES)
    )
    target_out[...], target_acc_out[...] = adagrad(target[...], target_acc[...], grads, learning_rate)
    grads = scatter(grad_query[...] * scale[...], one_hot(sid[1, 0], LANES))
    source_out[...], source_acc_out[...] = adagrad(
        moved[0:width, :], moved[width : width + 1, :], grads, learning_rate
    )


def last_update(sums, relation, relation_acc, relation_out, relation_acc_out):
    width, kinds = relation.shape
    for block in range(kinds // LANES):
        lanes = slice(block * LANES, (block + 1) * LANES)
        relation_out[:, lanes], relation_acc_out[:, lanes] = adagrad(
            relation[:, lanes], relation_acc[:, lanes], sums[block * width : (block + 1) * width, :], relation_rate
        )


def call(kernel, shapes, *operands, flops=0, fetch=False):
    outs = [jax.ShapeDtypeStruct(s, F32) for s in shapes]
    scratch, spec = [], VM
    if fetch:
        outs += [pltpu.VMEM(o.shape, o.dtype) for o in operands]
        outs[0] = pltpu.VMEM(shapes[0], F32)
        scratch = [pltpu.SemaphoreType.DMA((len(operands),))]
        spec = pl.BlockSpec(memory_space=pltpu.HBM)
    moved = sum(4 * int(np.prod(o.shape)) for o in outs) + sum(4 * o.size for o in operands)
    if fetch:
        operands = [pltpu.with_memory_space_constraint(o, pltpu.HBM) for o in operands]
    return pl.pallas_call(
        kernel,
        out_shape=outs,
        in_specs=[spec] * len(operands),
        out_specs=[VM] * len(outs),
        scratch_shapes=scratch,
        compiler_params=pltpu.CompilerParams(vmem_limit_bytes=40 * 2**20),
        cost_estimate=pl.CostEstimate(flops=flops, bytes_accessed=moved, transcendentals=0),
    )(*operands)


def exchange(blocks, groups):
    return lax.all_to_all(blocks, AXES, 0, 0, axis_index_groups=groups, tiled=True)


def spread(block, count):
    return jnp.broadcast_to(block[None], (count,) + block.shape)


def swap_cores(value):
    return lax.ppermute(value, "c", [(0, 1), (1, 0)])


def on_device(
    source_emb, source_state, target_emb, target_state, relation_emb, relation_state,
    sid, tid, kid, cnt, nid,
):
    source, target, relation = source_emb[0].T, target_emb[0].T, relation_emb.T
    cnt = cnt.transpose(1, 2, 0)
    width, kinds = relation.shape
    slots, negatives = sid.shape[-1], nid.shape[-1]
    table, row = (width, LANES), (1, LANES)
    edges, pairs = (width, slots), (negatives, slots)
    blocks = (width * kinds // 2 // LANES, LANES)
    work = 10**9
    moved, sid, source, tid, target, nid, kid, relation, cnt, _, target_state, relation_state = call(
        first_source, [(width + 8, LANES)],
        sid, source, tid, target, nid, kid, relation, cnt, source_state, target_state, relation_state[None],
        flops=2 * work, fetch=True,
    )
    count = lax.axis_size(BLK)
    moved = lax.ppermute(moved, BLK, [(i, (i + 1) % count) for i in range(count)])
    target, target_acc, total, right, sampled, scale = call(
        first_rest, [table, row, (2, width, kinds // 2), edges, (width, negatives), edges],
        source, target, target_state, relation, sid, tid, kid, nid, cnt, flops=4 * work,
    )
    query, pull, push, grad_query, typed, sent = call(
        second_edges, [edges, (1, slots), pairs, edges, edges, blocks],
        moved, right, sampled, scale, sid, kid, cnt, total, flops=2 * work,
    )
    received = swap_cores(sent)
    source, source_acc, target, target_acc, kept = call(
        second_rest, [table, row, table, row, blocks],
        moved, target, target_acc, scale, sid, tid, kid, nid, query, pull, push, grad_query, typed, total,
        flops=2 * work,
    )
    planes, lines = plane_groups(), line_groups()
    in_plane, in_line = len(planes[0]), len(lines[0])
    block = jnp.sum(exchange((kept + received).reshape(in_plane, 1, -1), planes), 0)
    block = jnp.sum(exchange(spread(block, in_line), lines), 0)
    halves = exchange(spread(block, in_plane), planes).reshape(blocks)
    sums = lax.all_gather(halves, "c", tiled=True)
    relation, relation_acc = call(
        last_update, [(width, kinds), (1, kinds)], sums, relation, relation_state
    )
    return (source.T[None], source_acc, target.T[None], target_acc, relation.T, relation_acc[0])


def solution(mesh):
    fine = Mesh(mesh.devices.reshape(SIZES), AXES)
    slab, sums = P(BLK, "l", None), P(BLK, "l")
    ids = P(None, BLK, "l", None)
    in_specs = (
        slab, sums, slab, sums, P(), P(), ids, ids, ids, P(None, BLK, "l"), P(None, BLK, "l", None, None),
    )
    out_specs = (slab, sums, slab, sums, P(), P())
    return jax.shard_map(
        on_device, mesh=fine, in_specs=in_specs, out_specs=out_specs, check_vma=False
    )
```

```python
import functools

import jax
import jax.numpy as jnp
import numpy as np
from jax import lax
from jax.experimental import pallas as pl
from jax.experimental.pallas import tpu as pltpu
from jax.sharding import Mesh
from jax.sharding import PartitionSpec as P

learning_rate = 0.1
relation_rate = 0.1

SIZES = (4, 2, 8, 2, 4)
AXES = ("x", "h", "y", "c", "l")
BLK = ("x", "h", "y", "c")
F32 = jnp.float32
VM = pl.BlockSpec(memory_space=pltpu.VMEM)
LANES = 128


def place(x, h, y, c, l):
    return (((x * 2 + h) * 8 + y) * 2 + c) * 4 + l


def plane_groups():
    first = [[place(x, h, y, 0, l) for x in range(4) for y in range(8)] for h in range(2) for l in range(4)]
    second = [[place(x, h, y, 1, l) for x in range(4) for h in range(2) for l in range(4)] for y in range(8)]
    return first + second


def line_groups():
    first = [[place(x, h, y, 0, l) for h in range(2) for l in range(4)] for x in range(4) for y in range(8)]
    second = [[place(x, h, y, 1, l) for y in range(8)] for x in range(4) for h in range(2) for l in range(4)]
    return first + second


def split(value):
    high = value.astype(jnp.bfloat16)
    return high, (value - high.astype(F32)).astype(jnp.bfloat16)


def product(left, right, dims=((1,), (0,))):
    return lax.dot_general(left, right, (dims, ((), ())), preferred_element_type=F32)


def product3(left, right, dims=((1,), (0,))):
    lh, ll = left
    rh, rl = right
    (a,), (b,) = dims
    return product(jnp.concatenate([lh, lh, ll], a), jnp.concatenate([rh, rl, rh], b), dims)


def one_hot(ids, count):
    rows = lax.broadcasted_iota(jnp.int32, (count, ids.shape[1]), 0)
    return (rows == ids).astype(F32).astype(jnp.bfloat16)


def gather(table, hot):
    high, low = split(table)
    if high.shape[1] == LANES:
        return product(jnp.concatenate([high, low], 1), jnp.concatenate([hot, hot], 0))
    return product(high, hot) + product(low, hot)


def scatter(values, hot):
    count = values.shape[0]
    both = product(jnp.concatenate(split(values), 0), hot, ((1,), (1,)))
    return both[:count] + both[count:]


def adagrad(weights, accum, grads, rate):
    fresh = accum + jnp.sum(grads * grads, axis=0, keepdims=True) / grads.shape[0]
    return weights - rate * grads * lax.rsqrt(fresh), fresh


def scores(query, right, sampled, count):
    slots, negatives = query.shape[1], sampled.shape[1]
    alive = (lax.broadcasted_iota(jnp.int32, (1, slots), 1) < count).astype(F32)
    positive = jnp.sum(query * right, axis=0, keepdims=True)
    negative = product3(split(sampled.T), split(query))
    pull = -alive * jax.nn.sigmoid(-positive)
    push = jax.nn.sigmoid(negative) * (alive / negatives)
    return pull, push


def target_grads(query, pull, push, target_hot, sample_hot):
    to_samples = product3(split(query), split(push), ((1,), (1,)))
    return scatter(pull * query, target_hot) + scatter(to_samples, sample_hot)


def bucket(left, right, sampled, scale, cnt):
    query = left * scale
    pull, push = scores(query, right, sampled, cnt)
    grad_query = pull * right + product3(split(sampled), split(push))
    return query, pull, push, grad_query


def first_source(*refs):
    count = (len(refs) - 2) // 2
    moved, arrived = refs[count], refs[-1]
    fetched = refs[count + 1 : -1]
    sid, source, tid, target, nid, kid, relation, cnt, source_acc = fetched[:9]
    copies = [pltpu.make_async_copy(refs[i], fetched[i], arrived.at[i]) for i in range(count)]
    for copy in copies:
        copy.start()
    for copy in copies:
        copy.wait()
    source_hot = one_hot(sid[0, 0], LANES)
    left = gather(source[...], source_hot)
    right = gather(target[...], one_hot(tid[0, 0], LANES))
    sampled = gather(target[...], one_hot(nid[0, 0, 0], LANES))
    scale = gather(relation[...], one_hot(kid[0, 0], relation.shape[1]))
    grad_query = bucket(left, right, sampled, scale, cnt[0, :, 0:1])[-1]
    grads = scatter(grad_query * scale, source_hot)
    rows, acc = adagrad(source[...], source_acc[...], grads, learning_rate)
    width = source.shape[0]
    moved[0:width, :] = rows
    moved[width : width + 8, :] = jnp.broadcast_to(acc, (8, LANES))


def first_rest(
    source, target, target_acc, relation, sid, tid, kid, nid, cnt,
    target_out, target_acc_out, total, right_out, sampled_out, scale_out,
):
    kind_hot = one_hot(kid[0, 0], relation.shape[1])
    target_hot, sample_hot = one_hot(tid[0, 0], LANES), one_hot(nid[0, 0, 0], LANES)
    left = gather(source[...], one_hot(sid[0, 0], LANES))
    query, pull, push, grad_query = bucket(
        left, gather(target[...], target_hot), gather(target[...], sample_hot), gather(relation[...], kind_hot),
        cnt[0, :, 0:1],
    )
    grads = target_grads(query, pull, push, target_hot, sample_hot)
    rows, acc = adagrad(target[...], target_acc[...], grads, learning_rate)
    target_out[...] = rows
    target_acc_out[...] = acc
    sums = scatter(grad_query * left, kind_hot)
    half = sums.shape[1] // 2
    total[0] = sums[:, :half]
    total[1] = sums[:, half:]
    right_out[...] = gather(rows, one_hot(tid[1, 0], LANES))
    sampled_out[...] = gather(rows, one_hot(nid[1, 0, 0], LANES))
    scale_out[...] = gather(relation[...], one_hot(kid[1, 0], relation.shape[1]))


def put_blocks(out, sums):
    width = sums.shape[0]
    for block in range(sums.shape[1] // LANES):
        out[block * width : (block + 1) * width, :] = sums[:, block * LANES : (block + 1) * LANES]


def second_edges(moved, right, sampled, scale, sid, kid, cnt, total, sent, kept):
    width = right.shape[0]
    left = gather(moved[0:width, :], one_hot(sid[1, 0], LANES))
    grad_query = bucket(left, right[...], sampled[...], scale[...], cnt[0, :, 1:2])[-1]
    typed = jnp.concatenate(split(grad_query * left), 0)
    me = lax.axis_index("c")
    half = total.shape[2]
    for blocks, mine in ((sent, 1 - me), (kept, me)):
        both = product(typed, one_hot(kid[1, 0] - mine * half, half), ((1,), (1,)))
        put_blocks(blocks, total[mine] + both[:width] + both[width:])


def second_rest(
    moved, target, target_acc, right, sampled, scale, sid, tid, nid, cnt,
    source_out, source_acc_out, target_out, target_acc_out,
):
    width = target.shape[0]
    source_hot = one_hot(sid[1, 0], LANES)
    left = gather(moved[0:width, :], source_hot)
    query, pull, push, grad_query = bucket(left, right[...], sampled[...], scale[...], cnt[0, :, 1:2])
    grads = target_grads(query, pull, push, one_hot(tid[1, 0], LANES), one_hot(nid[1, 0, 0], LANES))
    target_out[...], target_acc_out[...] = adagrad(target[...], target_acc[...], grads, learning_rate)
    grads = scatter(grad_query * scale[...], source_hot)
    source_out[...], source_acc_out[...] = adagrad(
        moved[0:width, :], moved[width : width + 1, :], grads, learning_rate
    )


def add_received(both, kept, out):
    out[...] = kept[...] + both[1 - lax.axis_index("c")]


def fold(parts, out, *, copies):
    block = out.shape[0] // copies
    count = parts.shape[0] // block
    total = parts[0:block, :]
    for i in range(1, count):
        total += parts[i * block : (i + 1) * block, :]
    for i in range(copies):
        out[i * block : (i + 1) * block, :] = total


def last_update(sums, relation, relation_acc, relation_out, relation_acc_out):
    width, kinds = relation.shape
    for block in range(kinds // LANES):
        lanes = slice(block * LANES, (block + 1) * LANES)
        relation_out[:, lanes], relation_acc_out[:, lanes] = adagrad(
            relation[:, lanes], relation_acc[:, lanes], sums[block * width : (block + 1) * width, :], relation_rate
        )


def call(kernel, shapes, *operands, flops=0, fetch=False, pinned=False):
    outs = [jax.ShapeDtypeStruct(s, F32) for s in shapes]
    scratch, spec = [], VM
    if pinned:
        outs = [pltpu.VMEM(s, F32) for s in shapes]
    if fetch:
        outs += [pltpu.VMEM(o.shape, o.dtype) for o in operands]
        outs[0] = pltpu.VMEM(shapes[0], F32)
        scratch = [pltpu.SemaphoreType.DMA((len(operands),))]
        spec = pl.BlockSpec(memory_space=pltpu.HBM)
    moved = sum(4 * int(np.prod(o.shape)) for o in outs) + sum(4 * o.size for o in operands)
    if fetch:
        operands = [pltpu.with_memory_space_constraint(o, pltpu.HBM) for o in operands]
    return pl.pallas_call(
        kernel,
        out_shape=outs,
        in_specs=[spec] * len(operands),
        out_specs=[VM] * len(outs),
        scratch_shapes=scratch,
        compiler_params=pltpu.CompilerParams(vmem_limit_bytes=16 * 2**20),
        cost_estimate=pl.CostEstimate(flops=flops, bytes_accessed=moved, transcendentals=0),
    )(*operands)


def in_vmem(value):
    return pltpu.with_memory_space_constraint(value, pltpu.VMEM)


def exchange(blocks, groups):
    return lax.all_to_all(blocks, AXES, 0, 0, axis_index_groups=groups, tiled=True)


def spread(block, count):
    return jnp.broadcast_to(block[None], (count,) + block.shape)


def swap_cores(value):
    return lax.ppermute(value, "c", [(0, 1), (1, 0)])


def on_device(
    source_emb, source_state, target_emb, target_state, relation_emb, relation_state,
    sid, tid, kid, cnt, nid,
):
    source, target, relation = source_emb[0].T, target_emb[0].T, relation_emb.T
    cnt = cnt.transpose(1, 2, 0)
    width, kinds = relation.shape
    slots, negatives = sid.shape[-1], nid.shape[-1]
    table, row = (width, LANES), (1, LANES)
    edges = (width, slots)
    blocks = (width * kinds // 2 // LANES, LANES)
    work = 10**9
    moved, sid, source, tid, target, nid, kid, relation, cnt, _, target_state, relation_state = call(
        first_source, [(width + 8, LANES)],
        sid, source, tid, target, nid, kid, relation, cnt, source_state, target_state, relation_state[None],
        flops=2 * work, fetch=True,
    )
    count = lax.axis_size(BLK)
    moved = lax.ppermute(moved, BLK, [(i, (i + 1) % count) for i in range(count)])
    target, target_acc, total, right, sampled, scale = call(
        first_rest, [table, row, (2, width, kinds // 2), edges, (width, negatives), edges],
        source, target, target_state, relation, sid, tid, kid, nid, cnt, flops=4 * work,
    )
    sent, kept = call(
        second_edges, [blocks, blocks], moved, right, sampled, scale, sid, kid, cnt, total, flops=2 * work
    )
    both = lax.all_gather(sent, "c")
    parts = call(add_received, [blocks], both, kept, pinned=True)[0]
    source, source_acc, target, target_acc = call(
        second_rest, [table, row, table, row],
        moved, target, target_acc, right, sampled, scale, sid, tid, nid, cnt, flops=4 * work,
    )
    planes, lines = plane_groups(), line_groups()
    in_plane, in_line = len(planes[0]), len(lines[0])
    share = blocks[0] // in_plane
    parts = exchange(parts.reshape(in_plane, 1, -1), planes).reshape(blocks)
    (block,) = call(functools.partial(fold, copies=in_line), [(share * in_line, LANES)], in_vmem(parts))
    block, source_acc = lax.optimization_barrier((block, source_acc))
    parts = exchange(block.reshape(in_line, 1, -1), lines).reshape(share * in_line, LANES)
    (block,) = call(functools.partial(fold, copies=in_plane), [blocks], in_vmem(parts))
    halves = exchange(block.reshape(in_plane, 1, -1), planes).reshape(blocks)
    sums = lax.all_gather(halves, "c", tiled=True)
    relation, relation_acc = call(
        last_update, [(width, kinds), (1, kinds)], sums, relation, relation_state
    )
    return (source.T[None], source_acc, target.T[None], target_acc, relation.T, relation_acc[0])


def solution(mesh):
    fine = Mesh(mesh.devices.reshape(SIZES), AXES)
    slab, sums = P(BLK, "l", None), P(BLK, "l")
    ids = P(None, BLK, "l", None)
    in_specs = (
        slab, sums, slab, sums, P(), P(), ids, ids, ids, P(None, BLK, "l"), P(None, BLK, "l", None, None),
    )
    out_specs = (slab, sums, slab, sums, P(), P())
    return jax.shard_map(
        on_device, mesh=fine, in_specs=in_specs, out_specs=out_specs, check_vma=False
    )
```

```python
import functools

import jax
import jax.numpy as jnp
import numpy as np
from jax import lax
from jax.experimental import pallas as pl
from jax.experimental.pallas import tpu as pltpu
from jax.sharding import Mesh
from jax.sharding import PartitionSpec as P

learning_rate = 0.1
relation_rate = 0.1

SIZES = (4, 2, 8, 2, 4)
AXES = ("x", "h", "y", "c", "l")
BLK = ("x", "h", "y", "c")
F32 = jnp.float32
VM = pl.BlockSpec(memory_space=pltpu.VMEM)
LANES = 128


def place(x, h, y, c, l):
    return (((x * 2 + h) * 8 + y) * 2 + c) * 4 + l


def plane_groups():
    first = [[place(x, h, y, 0, l) for x in range(4) for y in range(8)] for h in range(2) for l in range(4)]
    second = [[place(x, h, y, 1, l) for x in range(4) for h in range(2) for l in range(4)] for y in range(8)]
    return first + second


def line_groups():
    first = [[place(x, h, y, 0, l) for h in range(2) for l in range(4)] for x in range(4) for y in range(8)]
    second = [[place(x, h, y, 1, l) for y in range(8)] for x in range(4) for h in range(2) for l in range(4)]
    return first + second


def split(value):
    high = value.astype(jnp.bfloat16)
    return high, (value - high.astype(F32)).astype(jnp.bfloat16)


def product(left, right, dims=((1,), (0,))):
    return lax.dot_general(left, right, (dims, ((), ())), preferred_element_type=F32)


def product3(left, right, dims=((1,), (0,))):
    lh, ll = left
    rh, rl = right
    (a,), (b,) = dims
    return product(jnp.concatenate([lh, lh, ll], a), jnp.concatenate([rh, rl, rh], b), dims)


def one_hot(ids, count):
    rows = lax.broadcasted_iota(jnp.int32, (count, ids.shape[1]), 0)
    return (rows == ids).astype(F32).astype(jnp.bfloat16)


def gather(table, hot):
    high, low = split(table)
    if high.shape[1] == LANES:
        return product(jnp.concatenate([high, low], 1), jnp.concatenate([hot, hot], 0))
    return product(high, hot) + product(low, hot)


def scatter(values, hot):
    count = values.shape[0]
    both = product(jnp.concatenate(split(values), 0), hot, ((1,), (1,)))
    return both[:count] + both[count:]


def adagrad(weights, accum, grads, rate):
    fresh = accum + jnp.sum(grads * grads, axis=0, keepdims=True) / grads.shape[0]
    return weights - rate * grads * lax.rsqrt(fresh), fresh


def scores(query, right, sampled, count):
    slots, negatives = query.shape[1], sampled.shape[1]
    alive = (lax.broadcasted_iota(jnp.int32, (1, slots), 1) < count).astype(F32)
    positive = jnp.sum(query * right, axis=0, keepdims=True)
    negative = product3(split(sampled.T), split(query))
    pull = -alive * jax.nn.sigmoid(-positive)
    push = jax.nn.sigmoid(negative) * (alive / negatives)
    return pull, push


def target_grads(query, pull, push, target_hot, sample_hot):
    to_samples = product3(split(query), split(push), ((1,), (1,)))
    return scatter(pull * query, target_hot) + scatter(to_samples, sample_hot)


def bucket(left, right, sampled, scale, cnt):
    query = left * scale
    pull, push = scores(query, right, sampled, cnt)
    grad_query = pull * right + product3(split(sampled), split(push))
    return query, pull, push, grad_query


def first_source(*refs):
    count = (len(refs) - 2) // 2
    moved, arrived = refs[count], refs[-1]
    fetched = refs[count + 1 : -1]
    sid, source, tid, target, nid, kid, relation, cnt, source_acc = fetched[:9]
    copies = [pltpu.make_async_copy(refs[i], fetched[i], arrived.at[i]) for i in range(count)]
    for copy in copies:
        copy.start()
    for copy in copies:
        copy.wait()
    source_hot = one_hot(sid[0, 0], LANES)
    left = gather(source[...], source_hot)
    right = gather(target[...], one_hot(tid[0, 0], LANES))
    sampled = gather(target[...], one_hot(nid[0, 0, 0], LANES))
    scale = gather(relation[...], one_hot(kid[0, 0], relation.shape[1]))
    grad_query = bucket(left, right, sampled, scale, cnt[0, :, 0:1])[-1]
    grads = scatter(grad_query * scale, source_hot)
    rows, acc = adagrad(source[...], source_acc[...], grads, learning_rate)
    width = source.shape[0]
    moved[0:width, :] = rows
    moved[width : width + 8, :] = jnp.broadcast_to(acc, (8, LANES))


def first_rest(
    source, target, target_acc, relation, sid, tid, kid, nid, cnt,
    target_out, target_acc_out, total, right_out, sampled_out, scale_out,
):
    kind_hot = one_hot(kid[0, 0], relation.shape[1])
    target_hot, sample_hot = one_hot(tid[0, 0], LANES), one_hot(nid[0, 0, 0], LANES)
    left = gather(source[...], one_hot(sid[0, 0], LANES))
    query, pull, push, grad_query = bucket(
        left, gather(target[...], target_hot), gather(target[...], sample_hot), gather(relation[...], kind_hot),
        cnt[0, :, 0:1],
    )
    grads = target_grads(query, pull, push, target_hot, sample_hot)
    rows, acc = adagrad(target[...], target_acc[...], grads, learning_rate)
    target_out[...] = rows
    target_acc_out[...] = acc
    sums = scatter(grad_query * left, kind_hot)
    half = sums.shape[1] // 2
    total[0] = sums[:, :half]
    total[1] = sums[:, half:]
    right_out[...] = gather(rows, one_hot(tid[1, 0], LANES))
    sampled_out[...] = gather(rows, one_hot(nid[1, 0, 0], LANES))
    scale_out[...] = gather(relation[...], one_hot(kid[1, 0], relation.shape[1]))


def put_blocks(out, sums):
    width = sums.shape[0]
    for block in range(sums.shape[1] // LANES):
        out[block * width : (block + 1) * width, :] = sums[:, block * LANES : (block + 1) * LANES]


def second_edges(moved, right, sampled, scale, sid, kid, cnt, total, sent, kept):
    width = right.shape[0]
    left = gather(moved[0:width, :], one_hot(sid[1, 0], LANES))
    grad_query = bucket(left, right[...], sampled[...], scale[...], cnt[0, :, 1:2])[-1]
    typed = jnp.concatenate(split(grad_query * left), 0)
    me = lax.axis_index("c")
    half = total.shape[2]
    for blocks, mine in ((sent, 1 - me), (kept, me)):
        both = product(typed, one_hot(kid[1, 0] - mine * half, half), ((1,), (1,)))
        put_blocks(blocks, total[mine] + both[:width] + both[width:])


def second_rest(
    moved, target, target_acc, right, sampled, scale, sid, tid, nid, cnt,
    source_out, source_acc_out, target_out, target_acc_out,
):
    width = target.shape[0]
    source_hot = one_hot(sid[1, 0], LANES)
    left = gather(moved[0:width, :], source_hot)
    query, pull, push, grad_query = bucket(left, right[...], sampled[...], scale[...], cnt[0, :, 1:2])
    grads = target_grads(query, pull, push, one_hot(tid[1, 0], LANES), one_hot(nid[1, 0, 0], LANES))
    target_out[...], target_acc_out[...] = adagrad(target[...], target_acc[...], grads, learning_rate)
    grads = scatter(grad_query * scale[...], source_hot)
    source_out[...], source_acc_out[...] = adagrad(
        moved[0:width, :], moved[width : width + 1, :], grads, learning_rate
    )


def add_received(both, kept, out):
    out[...] = kept[...] + both[1 - lax.axis_index("c")]


def fold(parts, out, *, copies):
    block = out.shape[0] // copies
    count = parts.shape[0] // block
    total = parts[0:block, :]
    for i in range(1, count):
        total += parts[i * block : (i + 1) * block, :]
    for i in range(copies):
        out[i * block : (i + 1) * block, :] = total


def last_update(sums, relation, relation_acc, relation_out, relation_acc_out):
    width, kinds = relation.shape
    for block in range(kinds // LANES):
        lanes = slice(block * LANES, (block + 1) * LANES)
        relation_out[:, lanes], relation_acc_out[:, lanes] = adagrad(
            relation[:, lanes], relation_acc[:, lanes], sums[block * width : (block + 1) * width, :], relation_rate
        )


def call(kernel, shapes, *operands, flops=0, fetch=False, pinned=False):
    outs = [jax.ShapeDtypeStruct(s, F32) for s in shapes]
    scratch, spec = [], VM
    if pinned:
        outs = [pltpu.VMEM(s, F32) for s in shapes]
    if fetch:
        outs += [pltpu.VMEM(o.shape, o.dtype) for o in operands]
        outs[0] = pltpu.VMEM(shapes[0], F32)
        scratch = [pltpu.SemaphoreType.DMA((len(operands),))]
        spec = pl.BlockSpec(memory_space=pltpu.HBM)
    moved = sum(4 * int(np.prod(o.shape)) for o in outs) + sum(4 * o.size for o in operands)
    if fetch:
        operands = [pltpu.with_memory_space_constraint(o, pltpu.HBM) for o in operands]
    return pl.pallas_call(
        kernel,
        out_shape=outs,
        in_specs=[spec] * len(operands),
        out_specs=[VM] * len(outs),
        scratch_shapes=scratch,
        compiler_params=pltpu.CompilerParams(vmem_limit_bytes=16 * 2**20),
        cost_estimate=pl.CostEstimate(flops=flops, bytes_accessed=moved, transcendentals=0),
    )(*operands)


def in_vmem(value):
    return pltpu.with_memory_space_constraint(value, pltpu.VMEM)


def exchange(blocks, groups):
    return lax.all_to_all(blocks, AXES, 0, 0, axis_index_groups=groups, tiled=True)


def spread(block, count):
    return jnp.broadcast_to(block[None], (count,) + block.shape)


def swap_cores(value):
    return lax.ppermute(value, "c", [(0, 1), (1, 0)])


def on_device(
    source_emb, source_state, target_emb, target_state, relation_emb, relation_state,
    sid, tid, kid, cnt, nid,
):
    source, target, relation = source_emb[0].T, target_emb[0].T, relation_emb.T
    cnt = cnt.transpose(1, 2, 0)
    width, kinds = relation.shape
    slots, negatives = sid.shape[-1], nid.shape[-1]
    table, row = (width, LANES), (1, LANES)
    edges = (width, slots)
    blocks = (width * kinds // 2 // LANES, LANES)
    work = 10**9
    moved, sid, source, tid, target, nid, kid, relation, cnt, _, target_state, relation_state = call(
        first_source, [(width + 8, LANES)],
        sid, source, tid, target, nid, kid, relation, cnt, source_state, target_state, relation_state[None],
        flops=2 * work, fetch=True,
    )
    count = lax.axis_size(BLK)
    moved = lax.ppermute(moved, BLK, [(i, (i + 1) % count) for i in range(count)])
    target, target_acc, total, right, sampled, scale = call(
        first_rest, [table, row, (2, width, kinds // 2), edges, (width, negatives), edges],
        source, target, target_state, relation, sid, tid, kid, nid, cnt, flops=4 * work,
    )
    sent, kept = call(
        second_edges, [blocks, blocks], moved, right, sampled, scale, sid, kid, cnt, total, flops=2 * work
    )
    both = lax.all_gather(sent, "c")
    parts = call(add_received, [blocks], both, kept, pinned=True)[0]
    planes, lines = plane_groups(), line_groups()
    in_plane, in_line = len(planes[0]), len(lines[0])
    share = blocks[0] // in_plane
    parts = exchange(parts.reshape(in_plane, 1, -1), planes).reshape(blocks)
    (block,) = call(functools.partial(fold, copies=in_line), [(share * in_line, LANES)], in_vmem(parts))
    block, target_acc = lax.optimization_barrier((block, target_acc))
    parts = exchange(block.reshape(in_line, 1, -1), lines).reshape(share * in_line, LANES)
    source, source_acc, target, target_acc = call(
        second_rest, [table, row, table, row],
        moved, target, target_acc, right, sampled, scale, sid, tid, nid, cnt, flops=4 * work,
    )
    parts, source_acc = lax.optimization_barrier((parts, source_acc))
    (block,) = call(functools.partial(fold, copies=in_plane), [blocks], in_vmem(parts))
    halves = exchange(block.reshape(in_plane, 1, -1), planes).reshape(blocks)
    sums = lax.all_gather(halves, "c", tiled=True)
    relation, relation_acc = call(
        last_update, [(width, kinds), (1, kinds)], sums, relation, relation_state
    )
    return (source.T[None], source_acc, target.T[None], target_acc, relation.T, relation_acc[0])


def solution(mesh):
    fine = Mesh(mesh.devices.reshape(SIZES), AXES)
    slab, sums = P(BLK, "l", None), P(BLK, "l")
    ids = P(None, BLK, "l", None)
    in_specs = (
        slab, sums, slab, sums, P(), P(), ids, ids, ids, P(None, BLK, "l"), P(None, BLK, "l", None, None),
    )
    out_specs = (slab, sums, slab, sums, P(), P())
    return jax.shard_map(
        on_device, mesh=fine, in_specs=in_specs, out_specs=out_specs, check_vma=False
    )
```

```python
import functools

import jax
import jax.numpy as jnp
import numpy as np
from jax import lax
from jax.experimental import pallas as pl
from jax.experimental.pallas import tpu as pltpu
from jax.sharding import Mesh
from jax.sharding import PartitionSpec as P

learning_rate = 0.1
relation_rate = 0.1

SIZES = (4, 2, 8, 2, 4)
AXES = ("x", "h", "y", "c", "l")
BLK = ("x", "h", "y", "c")
F32 = jnp.float32
VM = pl.BlockSpec(memory_space=pltpu.VMEM)
LANES = 128


def place(x, h, y, c, l):
    return (((x * 2 + h) * 8 + y) * 2 + c) * 4 + l


def plane_groups():
    first = [[place(x, h, y, 0, l) for x in range(4) for y in range(8)] for h in range(2) for l in range(4)]
    second = [[place(x, h, y, 1, l) for x in range(4) for h in range(2) for l in range(4)] for y in range(8)]
    return first + second


def line_groups():
    first = [[place(x, h, y, 0, l) for h in range(2) for l in range(4)] for x in range(4) for y in range(8)]
    second = [[place(x, h, y, 1, l) for y in range(8)] for x in range(4) for h in range(2) for l in range(4)]
    return first + second


def split(value):
    high = value.astype(jnp.bfloat16)
    return high, (value - high.astype(F32)).astype(jnp.bfloat16)


def product(left, right, dims=((1,), (0,))):
    return lax.dot_general(left, right, (dims, ((), ())), preferred_element_type=F32)


def product3(left, right, dims=((1,), (0,))):
    lh, ll = left
    rh, rl = right
    (a,), (b,) = dims
    return product(jnp.concatenate([lh, lh, ll], a), jnp.concatenate([rh, rl, rh], b), dims)


def one_hot(ids, count):
    rows = lax.broadcasted_iota(jnp.int32, (count, ids.shape[1]), 0)
    return (rows == ids).astype(F32).astype(jnp.bfloat16)


def gather(table, hot):
    high, low = split(table)
    if high.shape[1] == LANES:
        return product(jnp.concatenate([high, low], 1), jnp.concatenate([hot, hot], 0))
    return product(high, hot) + product(low, hot)


def scatter(values, hot):
    count = values.shape[0]
    both = product(jnp.concatenate(split(values), 0), hot, ((1,), (1,)))
    return both[:count] + both[count:]


def adagrad(weights, accum, grads, rate):
    fresh = accum + jnp.sum(grads * grads, axis=0, keepdims=True) / grads.shape[0]
    return weights - rate * grads * lax.rsqrt(fresh), fresh


def scores(query, right, turned, count):
    slots, negatives = query.shape[1], turned.shape[0]
    alive = (lax.broadcasted_iota(jnp.int32, (1, slots), 1) < count).astype(F32)
    positive = jnp.sum(query * right, axis=0, keepdims=True)
    negative = product3(split(turned), split(query))
    pull = -alive * jax.nn.sigmoid(-positive)
    push = jax.nn.sigmoid(negative) * (alive / negatives)
    return pull, push


def target_grads(query, pull, push, target_hot, sample_hot):
    to_samples = product3(split(query), split(push), ((1,), (1,)))
    return scatter(pull * query, target_hot) + scatter(to_samples, sample_hot)


def bucket(left, right, sampled, scale, cnt, turned=None):
    query = left * scale
    pull, push = scores(query, right, sampled.T if turned is None else turned, cnt)
    grad_query = pull * right + product3(split(sampled), split(push))
    return query, pull, push, grad_query


def first_source(*refs):
    count = (len(refs) - 2) // 2
    moved, arrived = refs[count], refs[-1]
    fetched = refs[count + 1 : -1]
    sid, source, tid, target, nid, kid, relation, cnt, source_acc = fetched[:9]
    copies = [pltpu.make_async_copy(refs[i], fetched[i], arrived.at[i]) for i in range(count)]
    for copy in copies:
        copy.start()
    for copy in copies:
        copy.wait()
    source_hot = one_hot(sid[0, 0], LANES)
    left = gather(source[...], source_hot)
    right = gather(target[...], one_hot(tid[0, 0], LANES))
    sampled = gather(target[...], one_hot(nid[0, 0, 0], LANES))
    scale = gather(relation[...], one_hot(kid[0, 0], relation.shape[1]))
    grad_query = bucket(left, right, sampled, scale, cnt[0, :, 0:1])[-1]
    grads = scatter(grad_query * scale, source_hot)
    rows, acc = adagrad(source[...], source_acc[...], grads, learning_rate)
    width = source.shape[0]
    moved[0:width, :] = rows
    moved[width : width + 8, :] = jnp.broadcast_to(acc, (8, LANES))


def first_rest(
    source, target, target_acc, relation, sid, tid, kid, nid, cnt,
    target_out, target_acc_out, total, right_out, sampled_out, scale_out, turned_out,
):
    kind_hot = one_hot(kid[0, 0], relation.shape[1])
    target_hot, sample_hot = one_hot(tid[0, 0], LANES), one_hot(nid[0, 0, 0], LANES)
    left = gather(source[...], one_hot(sid[0, 0], LANES))
    query, pull, push, grad_query = bucket(
        left, gather(target[...], target_hot), gather(target[...], sample_hot), gather(relation[...], kind_hot),
        cnt[0, :, 0:1],
    )
    grads = target_grads(query, pull, push, target_hot, sample_hot)
    rows, acc = adagrad(target[...], target_acc[...], grads, learning_rate)
    target_out[...] = rows
    target_acc_out[...] = acc
    sums = scatter(grad_query * left, kind_hot)
    half = sums.shape[1] // 2
    total[0] = sums[:, :half]
    total[1] = sums[:, half:]
    right_out[...] = gather(rows, one_hot(tid[1, 0], LANES))
    sampled = gather(rows, one_hot(nid[1, 0, 0], LANES))
    sampled_out[...] = sampled
    turned_out[...] = sampled.T
    scale_out[...] = gather(relation[...], one_hot(kid[1, 0], relation.shape[1]))


def put_blocks(out, sums):
    width = sums.shape[0]
    for block in range(sums.shape[1] // LANES):
        out[block * width : (block + 1) * width, :] = sums[:, block * LANES : (block + 1) * LANES]


def second_edges(moved, right, sampled, turned, scale, sid, kid, cnt, total, sent, kept):
    width = right.shape[0]
    left = gather(moved[0:width, :], one_hot(sid[1, 0], LANES))
    grad_query = bucket(left, right[...], sampled[...], scale[...], cnt[0, :, 1:2], turned[...])[-1]
    typed = jnp.concatenate(split(grad_query * left), 0)
    me = lax.axis_index("c")
    half = total.shape[2]
    for blocks, mine in ((sent, 1 - me), (kept, me)):
        both = product(typed, one_hot(kid[1, 0] - mine * half, half), ((1,), (1,)))
        put_blocks(blocks, total[mine] + both[:width] + both[width:])


def second_rest(
    moved, target, target_acc, right, sampled, turned, scale, sid, tid, nid, cnt,
    source_out, source_acc_out, target_out, target_acc_out,
):
    width = target.shape[0]
    source_hot = one_hot(sid[1, 0], LANES)
    left = gather(moved[0:width, :], source_hot)
    query, pull, push, grad_query = bucket(left, right[...], sampled[...], scale[...], cnt[0, :, 1:2], turned[...])
    grads = target_grads(query, pull, push, one_hot(tid[1, 0], LANES), one_hot(nid[1, 0, 0], LANES))
    target_out[...], target_acc_out[...] = adagrad(target[...], target_acc[...], grads, learning_rate)
    grads = scatter(grad_query * scale[...], source_hot)
    source_out[...], source_acc_out[...] = adagrad(
        moved[0:width, :], moved[width : width + 1, :], grads, learning_rate
    )


def add_received(both, kept, out):
    out[...] = kept[...] + both[1 - lax.axis_index("c")]


def fold(parts, out, *, copies):
    block = out.shape[0] // copies
    count = parts.shape[0] // block
    total = parts[0:block, :]
    for i in range(1, count):
        total += parts[i * block : (i + 1) * block, :]
    for i in range(copies):
        out[i * block : (i + 1) * block, :] = total


def last_update(sums, relation, relation_acc, relation_out, relation_acc_out):
    width, kinds = relation.shape
    for block in range(kinds // LANES):
        lanes = slice(block * LANES, (block + 1) * LANES)
        relation_out[:, lanes], relation_acc_out[:, lanes] = adagrad(
            relation[:, lanes], relation_acc[:, lanes], sums[block * width : (block + 1) * width, :], relation_rate
        )


def call(kernel, shapes, *operands, flops=0, fetch=False, pinned=False):
    outs = [jax.ShapeDtypeStruct(s, F32) for s in shapes]
    scratch, spec = [], VM
    if pinned:
        outs = [pltpu.VMEM(s, F32) for s in shapes]
    if fetch:
        outs += [pltpu.VMEM(o.shape, o.dtype) for o in operands]
        outs[0] = pltpu.VMEM(shapes[0], F32)
        scratch = [pltpu.SemaphoreType.DMA((len(operands),))]
        spec = pl.BlockSpec(memory_space=pltpu.HBM)
    moved = sum(4 * int(np.prod(o.shape)) for o in outs) + sum(4 * o.size for o in operands)
    if fetch:
        operands = [pltpu.with_memory_space_constraint(o, pltpu.HBM) for o in operands]
    return pl.pallas_call(
        kernel,
        out_shape=outs,
        in_specs=[spec] * len(operands),
        out_specs=[VM] * len(outs),
        scratch_shapes=scratch,
        compiler_params=pltpu.CompilerParams(vmem_limit_bytes=16 * 2**20),
        cost_estimate=pl.CostEstimate(flops=flops, bytes_accessed=moved, transcendentals=0),
    )(*operands)


def in_vmem(value):
    return pltpu.with_memory_space_constraint(value, pltpu.VMEM)


def exchange(blocks, groups):
    return lax.all_to_all(blocks, AXES, 0, 0, axis_index_groups=groups, tiled=True)


def spread(block, count):
    return jnp.broadcast_to(block[None], (count,) + block.shape)


def swap_cores(value):
    return lax.ppermute(value, "c", [(0, 1), (1, 0)])


def on_device(
    source_emb, source_state, target_emb, target_state, relation_emb, relation_state,
    sid, tid, kid, cnt, nid,
):
    source, target, relation = source_emb[0].T, target_emb[0].T, relation_emb.T
    cnt = cnt.transpose(1, 2, 0)
    width, kinds = relation.shape
    slots, negatives = sid.shape[-1], nid.shape[-1]
    table, row = (width, LANES), (1, LANES)
    edges = (width, slots)
    blocks = (width * kinds // 2 // LANES, LANES)
    work = 10**9
    moved, sid, source, tid, target, nid, kid, relation, cnt, _, target_state, relation_state = call(
        first_source, [(width + 8, LANES)],
        sid, source, tid, target, nid, kid, relation, cnt, source_state, target_state, relation_state[None],
        flops=2 * work, fetch=True,
    )
    count = lax.axis_size(BLK)
    moved = lax.ppermute(moved, BLK, [(i, (i + 1) % count) for i in range(count)])
    target, target_acc, total, right, sampled, scale, turned = call(
        first_rest, [table, row, (2, width, kinds // 2), edges, (width, negatives), edges, (negatives, width)],
        source, target, target_state, relation, sid, tid, kid, nid, cnt, flops=4 * work,
    )
    sent, kept = call(
        second_edges, [blocks, blocks], moved, right, sampled, turned, scale, sid, kid, cnt, total, flops=2 * work
    )
    both = lax.all_gather(sent, "c")
    parts = call(add_received, [blocks], both, kept, pinned=True)[0]
    planes, lines = plane_groups(), line_groups()
    in_plane, in_line = len(planes[0]), len(lines[0])
    share = blocks[0] // in_plane
    parts = exchange(parts.reshape(in_plane, 1, -1), planes).reshape(blocks)
    (block,) = call(functools.partial(fold, copies=in_line), [(share * in_line, LANES)], in_vmem(parts))
    block, target_acc = lax.optimization_barrier((block, target_acc))
    parts = exchange(block.reshape(in_line, 1, -1), lines).reshape(share * in_line, LANES)
    source, source_acc, target, target_acc = call(
        second_rest, [table, row, table, row],
        moved, target, target_acc, right, sampled, turned, scale, sid, tid, nid, cnt, flops=4 * work,
    )
    parts, source_acc = lax.optimization_barrier((parts, source_acc))
    (block,) = call(functools.partial(fold, copies=in_plane), [blocks], in_vmem(parts))
    halves = exchange(block.reshape(in_plane, 1, -1), planes).reshape(blocks)
    sums = lax.all_gather(halves, "c", tiled=True)
    relation, relation_acc = call(
        last_update, [(width, kinds), (1, kinds)], sums, relation, relation_state
    )
    return (source.T[None], source_acc, target.T[None], target_acc, relation.T, relation_acc[0])


def solution(mesh):
    fine = Mesh(mesh.devices.reshape(SIZES), AXES)
    slab, sums = P(BLK, "l", None), P(BLK, "l")
    ids = P(None, BLK, "l", None)
    in_specs = (
        slab, sums, slab, sums, P(), P(), ids, ids, ids, P(None, BLK, "l"), P(None, BLK, "l", None, None),
    )
    out_specs = (slab, sums, slab, sums, P(), P())
    return jax.shard_map(
        on_device, mesh=fine, in_specs=in_specs, out_specs=out_specs, check_vma=False
    )
```
